32 devices in a mesh: tile: 8 (over z, x), lev: 4 (over y, core).
Axes of the slice: x: 2, y: 2, z: 4, core: 2. Of those that a mesh axis runs over, the one named last changes fastest.
Arguments:
- fields: float32 [2, 60, 1024, 128], P(None, 'lev', 'tile'), may hold values from -6 to 6
- wind_x: float32 [60, 1024, 128], P('lev', 'tile'), may hold values from -0.8 to 0.8
- wind_y: float32 [60, 1024, 128], P('lev', 'tile'), may hold values from -0.8 to 0.8
- diffusivity: float32 [60, 1024, 128], P('lev', 'tile'), may hold values from 0.02 to 0.3
- surface: float32 [8, 131072], P(None, ('tile', 'lev')), may hold values from -6 to 6
- cloud_list: int32 [131072], P(('tile', 'lev')), may hold values from -1 to 4095, as said below
- input_weight: bfloat16 [128, 512], replicated, may hold values from -0.5 to 0.5
- hidden_weight: bfloat16 [5, 512, 512], replicated, may hold values from -0.25 to 0.25
- output_weight: bfloat16 [512, 128], replicated, may hold values from -0.25 to 0.25
- clear_weight: bfloat16 [128, 128], replicated, may hold values from -0.5 to 0.5
Outputs:
- fields_out: float32 [2, 60, 131072], P(None, None, ('tile', 'lev'))
- surface_out: float32 [8, 131072], P(None, ('tile', 'lev'))
The draws below stay inside these ranges and needn't reach their ends.
Inputs may be any that keep to these rules, and one draw needn't show every extreme that they name: `cloud_list`: block d of 4096 entries belongs to the device of tile index d // 4 and lev index d % 4, whose columns are d * 4096 onward. Each block lists distinct local indices of cloudy columns in any order, then -1 to its end. Over the 8 blocks of one lev index, the numbers ceil(cloudy count / 512) sum to more than (3) * 8 and at most 32.
All inputs are finite; a program needn't handle non-finite values.
Results may differ from the reference program's by a relative error of at most 0.0055.
Values may be sent and summed in bfloat16 or wider, within the bound.
A program may use at most 128 MiB of HBM per device.

```python
import math
import jax
import jax.numpy as jnp
from jax import lax

LEVELS = 60
SURF = 8
HID = 512
HIDDEN_LAYERS = 5
NY = 128
F_IN = 128
NX = 1024
COLUMNS = 131072
COLS_DEV = 4096
BLOCK = 512
RECV_MOST = 4
N_TILE = 8
N_LEV = 4


def draw_cloud_list(key, part):
    tile_count = N_TILE
    groups = N_LEV
    cells = tile_count * tile_count
    keys = jax.random.split(jax.random.fold_in(key, 7), 5)
    weights = jax.random.randint(keys[0], (groups, tile_count, 1), 0, 3)
    orders = jax.vmap(lambda sub: jax.random.permutation(sub, cells))(jax.random.split(keys[1], groups))
    orders = orders.reshape(groups, tile_count, tile_count)
    cell_ids = jnp.arange(cells, dtype=jnp.int32).reshape(1, tile_count, tile_count)
    scores = (weights * (cells // 2) + orders) * cells + cell_ids
    ranking = jnp.argsort(jnp.argsort(scores.reshape(groups, cells), axis=1), axis=1)
    totals = RECV_MOST * tile_count - jax.random.randint(keys[2], (groups, 1), 0, tile_count)
    chosen = (ranking < totals).astype(jnp.int32).reshape(groups, tile_count, tile_count)
    block_counts = jnp.sum(chosen, axis=2)
    last_fill = jax.random.randint(keys[3], (groups, tile_count), 1, BLOCK + 1)
    cloudy_counts = jnp.where(block_counts > 0, (block_counts - 1) * BLOCK + last_fill, 0)
    picks = jax.vmap(lambda sub: jax.random.permutation(sub, COLS_DEV))(jax.random.split(keys[4], groups * tile_count))
    picks = picks.reshape(tile_count, groups, COLS_DEV)
    positions = jnp.arange(COLS_DEV, dtype=jnp.int32).reshape(1, 1, COLS_DEV)
    listed = jnp.where(positions < cloudy_counts.T[:, :, None], picks, -1)
    return listed.reshape(-1).astype(jnp.int32)


def level_of(stream_key, dims, pieces, smallest, top_value):
    gain = 1.0
    for dim, parts in pieces:
        heights = jax.random.uniform(jax.random.fold_in(jax.random.fold_in(stream_key, 6), dim), (parts,), jnp.float32, smallest / len(pieces), top_value / len(pieces))
        gain = gain * jnp.repeat(jnp.exp(heights), dims[dim] // parts).reshape((-1,) + (1,) * (len(dims) - 1 - dim))
    return gain


def centred(rng, dims, scale, most, pieces=(), kind=jnp.bfloat16):
    array = jax.random.normal(rng, dims, jnp.float32) * scale
    if len(pieces) > 0:
        array = level_of(rng, dims, pieces, -0.22, 0.18) * array
    return jnp.clip(array, min=-most, max=most).astype(kind)


def setup_inputs(seed: int = 0) -> dict:
    key_of = jax.random.split(jax.random.key(seed), 11)
    return {
        "fields": centred(key_of[0], (2, LEVELS, NX, NY), 1.0, 6.0, ((1, 4), (2, 8)), jnp.float32),
        "wind_x": jnp.clip(jax.random.uniform(key_of[1], (LEVELS, NX, NY), jnp.float32, -0.8, 0.8) * level_of(key_of[1], (LEVELS, NX, NY), ((0, 4), (1, 8)), -0.4, 0.0), -0.8, 0.8),
        "wind_y": jnp.clip(jax.random.uniform(key_of[2], (LEVELS, NX, NY), jnp.float32, -0.8, 0.8) * level_of(key_of[2], (LEVELS, NX, NY), ((0, 4), (1, 8)), -0.4, 0.0), -0.8, 0.8),
        "diffusivity": jnp.clip(jnp.exp(math.log(0.3) - 2.7080503 * jax.random.uniform(key_of[3], (LEVELS, NX, NY), jnp.float32) ** level_of(key_of[3], (LEVELS, NX, NY), ((0, 4), (1, 8)), -0.2, 0.2)), 0.02, 0.3),
        "surface": centred(key_of[4], (SURF, COLUMNS), 1.0, 6.0, ((1, 32),), jnp.float32),
        "cloud_list": draw_cloud_list(jax.random.fold_in(key_of[10], 71), 0),
        "input_weight": centred(key_of[6], (F_IN, HID), F_IN ** -0.5, 0.5),
        "hidden_weight": centred(key_of[7], (HIDDEN_LAYERS, HID, HID), HID ** -0.5, 0.25),
        "output_weight": centred(key_of[8], (HID, F_IN), HID ** -0.5, 0.25),
        "clear_weight": centred(key_of[9], (F_IN, F_IN), F_IN ** -0.5, 0.5),
    }


def rate(field, wind_east, wind_north, diffuse):
    east_cell = jnp.roll(field, -1, axis=2)
    west_cell = jnp.roll(field, 1, axis=2)
    zero_edge = jnp.zeros_like(field[..., :1])
    north_cell = jnp.concatenate([field[..., 1:], zero_edge], axis=-1)
    south_cell = jnp.concatenate([zero_edge, field[..., :-1]], axis=-1)
    spread = east_cell + west_cell + north_cell + south_cell - 4.0 * field
    carried = wind_east * (east_cell - west_cell) + wind_north * (north_cell - south_cell)
    return diffuse * spread - 0.5 * carried


def physics_rows(batch, input_weight, hidden_weight, output_weight):
    stream = jax.nn.silu(jnp.dot(batch.astype(jnp.float32), input_weight.astype(jnp.float32)))
    for layer_index in range(HIDDEN_LAYERS):
        operand = stream.astype(jnp.bfloat16).astype(jnp.float32)
        stream = stream + jax.nn.silu(jnp.dot(operand, hidden_weight[layer_index].astype(jnp.float32)))
    operand = stream.astype(jnp.bfloat16).astype(jnp.float32)
    return jnp.dot(operand, output_weight.astype(jnp.float32)).astype(jnp.bfloat16)


def reference(fields, wind_x, wind_y, diffusivity, surface, cloud_list, input_weight, hidden_weight, output_weight, clear_weight):
    section_one = fields + rate(fields, wind_x, wind_y, diffusivity) / 3.0
    section_two = fields + 0.5 * rate(section_one, wind_x, wind_y, diffusivity)
    advected = fields + rate(section_two, wind_x, wind_y, diffusivity)
    columns = advected.reshape(2, LEVELS, COLUMNS)
    features = jnp.concatenate([columns.reshape(2 * LEVELS, COLUMNS), surface], axis=0).astype(jnp.bfloat16).T
    clear_part = jnp.dot(features.astype(jnp.float32), clear_weight.astype(jnp.float32))
    base_index = (jnp.arange(COLUMNS, dtype=jnp.int32) // COLS_DEV) * COLS_DEV
    target = jnp.where(cloud_list >= 0, base_index + cloud_list, COLUMNS).astype(jnp.int32)
    cloudy = jnp.zeros((COLUMNS + 1,), dtype=jnp.int32).at[target].set(1)[:COLUMNS]
    physics = lax.map(lambda batch: physics_rows(batch, input_weight, hidden_weight, output_weight),
                      features.reshape(COLUMNS // COLS_DEV, COLS_DEV, F_IN)).reshape(COLUMNS, F_IN)
    tendency = (clear_part + jnp.where(cloudy[:, None] > 0, physics.astype(jnp.float32), 0.0)).astype(jnp.bfloat16)
    tend_cols = tendency.astype(jnp.float32).T
    fields_out = columns + tend_cols[:2 * LEVELS].reshape(2, LEVELS, COLUMNS)
    surface_out = surface + tend_cols[2 * LEVELS:]
    return fields_out, surface_out
```

```python
import functools

import numpy as np
import jax
import jax.numpy as jnp
from jax import lax
from jax.experimental import pallas as pl
from jax.experimental.pallas import tpu as pltpu
from jax.sharding import PartitionSpec as P

F32 = jnp.float32
BF16 = jnp.bfloat16
ROWS = 8
VMEM_LIMIT = 56 * 1024 * 1024


def advect_kernel(
    tiles, levs, lb, lp, nx, ny,
    f_hbm, wx_hbm, wy_hbm, d_hbm, out_ref,
    fv, wv, padded, coef, edge_out, edge_in, outbox,
    load_sem, halo_send, halo_recv, part_send, part_recv,
):
    tile = lax.axis_index("tile")
    me = lax.axis_index("lev")
    right = lax.rem(tile + 1, tiles)
    left = lax.rem(tile + tiles - 1, tiles)
    mine = nx // levs
    steps = mine // ROWS
    group = 2 * lp

    loads = [pltpu.make_async_copy(f_hbm, fv.at[pl.ds(0, 2 * lb * nx)], load_sem.at[0])]
    for i, ref in enumerate((wx_hbm, wy_hbm, d_hbm)):
        loads.append(
            pltpu.make_async_copy(ref, wv.at[pl.ds(i * lp * nx, lb * nx)], load_sem.at[i + 1])
        )
    for copy in loads:
        copy.start()

    barrier = pltpu.get_barrier_semaphore()
    for near in (left, right):
        pl.semaphore_signal(
            barrier, inc=1, device_id={"tile": near}, device_id_type=pl.DeviceIdType.MESH
        )
    for o in range(1, levs):
        pl.semaphore_signal(
            barrier, inc=1, device_id={"lev": lax.rem(me + o, levs)},
            device_id_type=pl.DeviceIdType.MESH,
        )

    extra = lp - lb
    if extra:
        fv[pl.ds(2 * lb * nx, extra * nx), :] = jnp.zeros((extra * nx, ny), F32)
        for i in range(3):
            wv[pl.ds((i * lp + lb) * nx, extra * nx), :] = jnp.zeros((extra * nx, ny), F32)

    lane = lax.broadcasted_iota(jnp.int32, (lp, ny), 1)
    north_ok = lane < ny - 1
    south_ok = lane > 0

    def level_rows(ref, first, x):
        parts = [ref[pl.ds((first + 8 * h) * nx + x, 8, stride=nx), :] for h in range(lp // 8)]
        return jnp.concatenate(parts, axis=0)

    def convert(x):
        for v in range(2):
            padded[x + 3, v * lp : (v + 1) * lp, :] = level_rows(fv, v * lb, x)

    def set_coef(row, wx, wy, d):
        wx = 0.5 * wx
        wy = 0.5 * wy
        coef[row, 0] = d - wx
        coef[row, 1] = d + wx
        coef[row, 2] = jnp.where(north_ok, d - wy, 0.0)
        coef[row, 3] = jnp.where(south_ok, d + wy, 0.0)
        coef[row, 4] = 4.0 * d

    for copy in loads:
        copy.wait()
    for x in (0, 1, 2, nx - 3, nx - 2, nx - 1):
        convert(x)
    for side, first in ((0, 0), (1, nx - 2)):
        for r in range(2):
            for i in range(3):
                edge_out[side, r * 3 + i] = level_rows(wv, i * lp, first + r)

    pl.semaphore_wait(barrier, 2 + levs - 1)

    def halo_copy(src, dst, index, near):
        return pltpu.make_async_remote_copy(
            src_ref=src, dst_ref=dst, send_sem=halo_send.at[index], recv_sem=halo_recv.at[index],
            device_id={"tile": near}, device_id_type=pl.DeviceIdType.MESH,
        )

    halos = [
        halo_copy(padded.at[pl.ds(nx, 3)], padded.at[pl.ds(0, 3)], 0, right),
        halo_copy(padded.at[pl.ds(3, 3)], padded.at[pl.ds(nx + 3, 3)], 1, left),
        halo_copy(edge_out.at[1], edge_in.at[0], 2, right),
        halo_copy(edge_out.at[0], edge_in.at[1], 3, left),
    ]
    for copy in halos:
        copy.start()

    @pl.loop(3, nx - 3)
    def _(x):
        convert(x)

    @pl.loop(0, nx)
    def _(x):
        set_coef(x + 2, *(level_rows(wv, i * lp, x) for i in range(3)))

    def rate(c, e, w, row):
        north = pltpu.roll(c, ny - 1, axis=1)
        south = pltpu.roll(c, 1, axis=1)
        return (
            coef[row, 0] * e + coef[row, 1] * w + coef[row, 2] * north + coef[row, 3] * south
            - coef[row, 4] * c
        )

    def section(x0, save):
        for v in range(2):
            lo, hi = v * lp, (v + 1) * lp
            f = [padded[x0 + i, lo:hi, :] for i in range(2)]
            one = []
            two = []
            for r in range(ROWS + 4):
                f.append(padded[x0 + r + 2, lo:hi, :])
                one.append(f[r + 1] + rate(f[r + 1], f[r + 2], f[r], x0 + r) * (1.0 / 3.0))
                if r >= 2:
                    two.append(
                        f[r] + 0.5 * rate(one[r - 1], one[r], one[r - 2], x0 + r - 1)
                    )
                if r >= 4:
                    done = f[r - 1] + rate(two[r - 3], two[r - 2], two[r - 4], x0 + r - 2)
                    save(r - 4, lo, done.astype(BF16))

    def part_copy(k, o, source):
        return pltpu.make_async_remote_copy(
            src_ref=outbox.at[o - 1, pl.ds(k * ROWS, ROWS)],
            dst_ref=out_ref.at[pl.ds(k * ROWS, ROWS), pl.ds(pl.multiple_of(source * group, group), group)],
            send_sem=part_send.at[k, o - 1],
            recv_sem=part_recv.at[k, o - 1],
            device_id={"lev": lax.rem(me + o, levs)},
            device_id_type=pl.DeviceIdType.MESH,
        )

    def step(k):
        @pl.loop(1, levs)
        def _(o):
            def save(r, lo, value):
                outbox[o - 1, k * ROWS + r, lo : lo + lp, :] = value

            section(lax.rem(me + o, levs) * mine + k * ROWS, save)
            part_copy(k, o, me).start()

    def own(k):
        base = pl.multiple_of(me * group, group)

        def save(r, lo, value):
            out_ref[k * ROWS + r, pl.ds(base + lo, lp), :] = value

        section(me * mine + k * ROWS, save)

    @pl.loop(1, steps - 1)
    def _(k):
        step(k)

    for copy in halos:
        copy.wait()
    for side, first in ((0, 0), (1, nx + 2)):
        for r in range(2):
            set_coef(first + r, *(edge_in[side, r * 3 + i] for i in range(3)))

    @pl.loop(0, 2)
    def _(i):
        step(i * (steps - 1))

    @pl.loop(0, steps)
    def _(k):
        own(k)

    @pl.loop(0, steps)
    def _(k):
        @pl.loop(1, levs)
        def _(o):
            part_copy(k, o, me).wait_send()
            part_copy(k, o, lax.rem(me + levs - o, levs)).wait_recv()


def nt(a, b):
    return lax.dot_general(a, b, (((1,), (1,)), ((), ())), preferred_element_type=F32)


def silu(v):
    h = 0.5 * v
    return h * jnp.tanh(h) + h


def physics_kernel(
    rows, lanes, groups, levels, level_pad, layers,
    feat_ref, surf_ref, cloud_ref, pin_ref, pout_ref, move_ref, iw_ref, hw_ref, ow_ref, cw_ref,
    fields_ref, surface_ref,
    mask, iw, ow, cw,
):
    step = pl.program_id(0)

    @pl.when(step == 0)
    def _():
        listed = cloud_ref[...]
        count = listed.shape[1]
        high = lax.broadcasted_iota(jnp.int32, (mask.shape[0], count), 0)
        low = lax.broadcasted_iota(jnp.int32, (lanes, count), 0)
        top = jnp.right_shift(listed, int(lanes).bit_length() - 1)
        hot_high = jnp.where(high == top, 1.0, 0.0).astype(BF16)
        hot_low = jnp.where(low == jnp.bitwise_and(listed, lanes - 1), 1.0, 0.0).astype(BF16)
        mask[...] = nt(hot_high, hot_low)
        iw[...] = jnp.dot(pin_ref[...], iw_ref[...], preferred_element_type=F32).astype(BF16)
        ow[...] = nt(pout_ref[...], ow_ref[...]).astype(BF16)
        turned = nt(pout_ref[...], cw_ref[...]).astype(BF16)
        cw[: turned.shape[0], :] = nt(turned, pin_ref[...]).astype(BF16)
        cw[turned.shape[0] :, :] = move_ref[...]

    surf = surf_ref[...]
    surf16 = surf.astype(BF16)
    tail = jnp.concatenate([surf16, jnp.zeros_like(surf16)], axis=0)
    feat = jnp.concatenate([feat_ref[r] for r in range(rows)], axis=1)
    feat = jnp.concatenate([feat, tail], axis=0)

    half = rows * lanes // 2
    streams = []
    for s in range(2):
        piece = feat[:, s * half : (s + 1) * half]
        streams.append(
            silu(lax.dot_general(piece, iw[...], (((0,), (0,)), ((), ())), preferred_element_type=F32))
        )
    for layer in range(layers):
        for s in range(2):
            streams[s] = streams[s] + silu(
                jnp.dot(streams[s].astype(BF16), hw_ref[layer], preferred_element_type=F32)
            )
    both = jnp.dot(cw[...], feat, preferred_element_type=F32)
    out_rows = ow.shape[0]
    for s in range(2):
        physics = nt(ow[...], streams[s].astype(BF16)).astype(BF16).astype(F32)
        keep = jnp.concatenate(
            [mask[pl.ds(step * rows + s * (rows // 2) + r, 1), :] for r in range(rows // 2)], axis=1
        )
        at = slice(s * half, (s + 1) * half)
        tend = both[:out_rows, at] + jnp.where(keep > 0.5, physics, 0.0)
        tend = tend.astype(BF16).astype(F32)
        for v in range(2):
            first = v * level_pad
            fields_ref[v, :, at] = (
                both[out_rows + first : out_rows + first + levels, at]
                + tend[first : first + levels]
            )
        surface_ref[:, at] = surf[:, at] + tend[2 * level_pad : 2 * level_pad + surf.shape[0]]


def orders(levs, lb, lp, levels, level_pad, surf, features):
    size_in = levs * 2 * lp + 2 * surf
    size_out = 2 * level_pad + 2 * surf
    pin = np.zeros((size_in, features), np.float32)
    pout = np.zeros((size_out, features), np.float32)
    for v in range(2):
        for level in range(levels):
            j, l = divmod(level, lb)
            pin[j * 2 * lp + v * lp + l, v * levels + level] = 1.0
            pout[v * level_pad + level, v * levels + level] = 1.0
    for s in range(surf):
        pin[levs * 2 * lp + s, 2 * levels + s] = 1.0
        pout[2 * level_pad + s, 2 * levels + s] = 1.0
    return pin, pout, pout @ pin.T


def local(
    tiles, levs,
    fields, wind_x, wind_y, diffusivity, surface, cloud_list,
    input_weight, hidden_weight, output_weight, clear_weight,
):
    _, lb, nx, ny = fields.shape
    lp = -(-lb // 8) * 8
    levels = lb * levs
    level_pad = -(-levels // 8) * 8
    mine = nx // levs
    group = 2 * lp
    any_spec = pl.BlockSpec(memory_space=pl.ANY)
    vmem_spec = pl.BlockSpec(memory_space=pltpu.VMEM)
    parts = mine // ROWS
    feats = pl.pallas_call(
        functools.partial(advect_kernel, tiles, levs, lb, lp, nx, ny),
        out_shape=jax.ShapeDtypeStruct((mine, levs * group, ny), BF16),
        in_specs=[any_spec] * 4,
        out_specs=vmem_spec,
        scratch_shapes=[
            pltpu.VMEM(((2 * lb + lp - lb) * nx, ny), F32),
            pltpu.VMEM((3 * lp * nx, ny), F32),
            pltpu.VMEM((nx + 6, group, ny), F32),
            pltpu.VMEM((nx + 4, 5, lp, ny), F32),
            pltpu.VMEM((2, 6, lp, ny), F32),
            pltpu.VMEM((2, 6, lp, ny), F32),
            pltpu.VMEM((levs - 1, mine, group, ny), BF16),
            pltpu.SemaphoreType.DMA((4,)),
            pltpu.SemaphoreType.DMA((4,)),
            pltpu.SemaphoreType.DMA((4,)),
            pltpu.SemaphoreType.DMA((parts, levs - 1)),
            pltpu.SemaphoreType.DMA((parts, levs - 1)),
        ],
        compiler_params=pltpu.CompilerParams(
            collective_id=0, has_side_effects=True, vmem_limit_bytes=VMEM_LIMIT
        ),
        name="advect",
    )(
        fields.reshape(2 * lb * nx, ny),
        wind_x.reshape(lb * nx, ny),
        wind_y.reshape(lb * nx, ny),
        diffusivity.reshape(lb * nx, ny),
    )

    surf, cols = surface.shape
    features, hid = input_weight.shape
    layers = hidden_weight.shape[0]
    pin, pout, move = (
        jnp.asarray(m, BF16) for m in orders(levs, lb, lp, levels, level_pad, surf, features)
    )
    size_in, size_out = pin.shape[0], pout.shape[0]
    rows = 8
    wide = rows * ny
    return pl.pallas_call(
        functools.partial(physics_kernel, rows, ny, levs, levels, level_pad, layers),
        grid=(mine // rows,),
        out_shape=(
            jax.ShapeDtypeStruct((2, levels, cols), F32),
            jax.ShapeDtypeStruct((surf, cols), F32),
        ),
        in_specs=[
            pl.BlockSpec((rows, levs * group, ny), lambda i: (i, 0, 0)),
            pl.BlockSpec((surf, wide), lambda i: (0, i)),
        ] + [vmem_spec] * 8,
        out_specs=(
            pl.BlockSpec((2, levels, wide), lambda i: (0, 0, i)),
            pl.BlockSpec((surf, wide), lambda i: (0, i)),
        ),
        scratch_shapes=[
            pltpu.VMEM((mine, ny), F32),
            pltpu.VMEM((size_in, hid), BF16),
            pltpu.VMEM((size_out, hid), BF16),
            pltpu.VMEM((2 * size_out, size_in), BF16),
        ],
        compiler_params=pltpu.CompilerParams(vmem_limit_bytes=VMEM_LIMIT),
        name="physics",
    )(
        feats, surface, cloud_list.reshape(1, -1), pin, pout, move,
        input_weight, hidden_weight, output_weight, clear_weight,
    )


def solution(mesh):
    return jax.shard_map(
        functools.partial(local, mesh.shape["tile"], mesh.shape["lev"]),
        mesh=mesh,
        in_specs=(
            P(None, "lev", "tile", None),
            P("lev", "tile", None),
            P("lev", "tile", None),
            P("lev", "tile", None),
            P(None, ("tile", "lev")),
            P(("tile", "lev")),
            P(),
            P(),
            P(),
            P(),
        ),
        out_specs=(P(None, None, ("tile", "lev")), P(None, ("tile", "lev"))),
        check_vma=False,
    )
```

```python
import functools

import numpy as np
import jax
import jax.numpy as jnp
from jax import lax
from jax.experimental import pallas as pl
from jax.experimental.pallas import tpu as pltpu
from jax.sharding import PartitionSpec as P

F32 = jnp.float32
BF16 = jnp.bfloat16
ROWS = 8
ADVECT_VMEM = 58 * 1024 * 1024
PHYSICS_VMEM = 58 * 1024 * 1024


def advect_kernel(
    tiles, levs, lb, lp, nx, ny,
    f_hbm, wx_hbm, wy_hbm, d_hbm, *refs,
):
    small_hbm, refs = refs[:7], refs[7:]
    out_ref, mask, iw, ow, cw = refs[:5]
    small, refs = refs[5:12], refs[12:]
    fv, wv, padded, coef, edge_out, edge_in, outbox, load_sem, small_sem = refs[:9]
    halo_send, halo_recv, part_send, part_recv = refs[9:]
    tile = lax.axis_index("tile")
    me = lax.axis_index("lev")
    right = lax.rem(tile + 1, tiles)
    left = lax.rem(tile + tiles - 1, tiles)
    mine = nx // levs
    steps = mine // ROWS
    group = 2 * lp

    loads = [pltpu.make_async_copy(f_hbm, fv.at[pl.ds(0, 2 * lb * nx)], load_sem.at[0])]
    for i, ref in enumerate((wx_hbm, wy_hbm, d_hbm)):
        loads.append(
            pltpu.make_async_copy(ref, wv.at[pl.ds(i * lp * nx, lb * nx)], load_sem.at[i + 1])
        )
    extras = [
        pltpu.make_async_copy(src, dst, small_sem.at[i])
        for i, (src, dst) in enumerate(zip(small_hbm, small))
    ]
    for copy in loads + extras:
        copy.start()

    barrier = pltpu.get_barrier_semaphore()
    for near in (left, right):
        pl.semaphore_signal(
            barrier, inc=1, device_id={"tile": near}, device_id_type=pl.DeviceIdType.MESH
        )
    for o in range(1, levs):
        pl.semaphore_signal(
            barrier, inc=1, device_id={"lev": lax.rem(me + o, levs)},
            device_id_type=pl.DeviceIdType.MESH,
        )

    extra = lp - lb
    if extra:
        fv[pl.ds(2 * lb * nx, extra * nx), :] = jnp.zeros((extra * nx, ny), F32)
        for i in range(3):
            wv[pl.ds((i * lp + lb) * nx, extra * nx), :] = jnp.zeros((extra * nx, ny), F32)

    lane = lax.broadcasted_iota(jnp.int32, (lp, ny), 1)
    north_ok = lane < ny - 1
    south_ok = lane > 0

    def level_rows(ref, first, x):
        parts = [ref[pl.ds((first + 8 * h) * nx + x, 8, stride=nx), :] for h in range(lp // 8)]
        return jnp.concatenate(parts, axis=0)

    def convert(x):
        for v in range(2):
            padded[x + 3, v * lp : (v + 1) * lp, :] = level_rows(fv, v * lb, x)

    def set_coef(row, wx, wy, d):
        wx = 0.5 * wx
        wy = 0.5 * wy
        coef[row, 0] = d - wx
        coef[row, 1] = d + wx
        coef[row, 2] = jnp.where(north_ok, d - wy, 0.0)
        coef[row, 3] = jnp.where(south_ok, d + wy, 0.0)
        coef[row, 4] = 4.0 * d

    for copy in loads:
        copy.wait()
    for x in (0, 1, 2, nx - 3, nx - 2, nx - 1):
        convert(x)
    for side, first in ((0, 0), (1, nx - 2)):
        for r in range(2):
            for i in range(3):
                edge_out[side, r * 3 + i] = level_rows(wv, i * lp, first + r)

    pl.semaphore_wait(barrier, 2 + levs - 1)

    def halo_copy(src, dst, index, near):
        return pltpu.make_async_remote_copy(
            src_ref=src, dst_ref=dst, send_sem=halo_send.at[index], recv_sem=halo_recv.at[index],
            device_id={"tile": near}, device_id_type=pl.DeviceIdType.MESH,
        )

    halos = [
        halo_copy(padded.at[pl.ds(nx, 3)], padded.at[pl.ds(0, 3)], 0, right),
        halo_copy(padded.at[pl.ds(3, 3)], padded.at[pl.ds(nx + 3, 3)], 1, left),
        halo_copy(edge_out.at[1], edge_in.at[0], 2, right),
        halo_copy(edge_out.at[0], edge_in.at[1], 3, left),
    ]
    for copy in halos:
        copy.start()

    @pl.loop(0, nx // 8)
    def _(b):
        for r in range(8):
            x = b * 8 + r
            set_coef(x + 2, *(level_rows(wv, i * lp, x) for i in range(3)))

    @pl.loop(0, (nx - 6) // 2, unroll=4)
    def _(b):
        for r in range(2):
            convert(3 + b * 2 + r)

    def rate(c, e, w, row):
        north = pltpu.roll(c, ny - 1, axis=1)
        south = pltpu.roll(c, 1, axis=1)
        return (
            coef[row, 0] * e + coef[row, 1] * w + coef[row, 2] * north + coef[row, 3] * south
            - coef[row, 4] * c
        )

    def section(x0, save):
        for v in range(2):
            lo, hi = v * lp, (v + 1) * lp
            f = [padded[x0 + i, lo:hi, :] for i in range(2)]
            one = []
            two = []
            for r in range(ROWS + 4):
                f.append(padded[x0 + r + 2, lo:hi, :])
                one.append(f[r + 1] + rate(f[r + 1], f[r + 2], f[r], x0 + r) * (1.0 / 3.0))
                if r >= 2:
                    two.append(
                        f[r] + 0.5 * rate(one[r - 1], one[r], one[r - 2], x0 + r - 1)
                    )
                if r >= 4:
                    done = f[r - 1] + rate(two[r - 3], two[r - 2], two[r - 4], x0 + r - 2)
                    save(r - 4, lo, done.astype(BF16))

    pair = 2 if levs % 2 == 0 else 1
    chips = levs // pair
    high, low = me // pair, lax.rem(me, pair)

    def peer(o, sign):
        far = lax.rem(high + (o // pair if sign > 0 else chips - o // pair), chips)
        return far * pair + lax.rem(low + (o % pair if sign > 0 else pair - o % pair), pair)

    def part_copy(k, o, source):
        return pltpu.make_async_remote_copy(
            src_ref=outbox.at[o - 1, pl.ds(k * ROWS, ROWS)],
            dst_ref=out_ref.at[pl.ds(k * ROWS, ROWS), pl.ds(pl.multiple_of(source * group, group), group)],
            send_sem=part_send.at[k, o - 1],
            recv_sem=part_recv.at[k, o - 1],
            device_id={"lev": peer(o, 1)},
            device_id_type=pl.DeviceIdType.MESH,
        )

    def step(k, o):
        def save(r, lo, value):
            outbox[o - 1, k * ROWS + r, lo : lo + lp, :] = value

        section(peer(o, 1) * mine + k * ROWS, save)
        part_copy(k, o, me).start()

    def own(k):
        base = pl.multiple_of(me * group, group)

        def save(r, lo, value):
            out_ref[k * ROWS + r, pl.ds(base + lo, lp), :] = value

        section(me * mine + k * ROWS, save)

    @pl.loop(1, steps - 1)
    def _(k):
        @pl.loop(pair, levs)
        def _(o):
            step(k, o)

    for copy in halos:
        copy.wait()
    for side, first in ((0, 0), (1, nx + 2)):
        for r in range(2):
            set_coef(first + r, *(edge_in[side, r * 3 + i] for i in range(3)))

    @pl.loop(0, 2)
    def _(i):
        @pl.loop(pair, levs)
        def _(o):
            step(i * (steps - 1), o)

    @pl.loop(0, steps)
    def _(k):
        @pl.loop(1, pair)
        def _(o):
            step(k, o)

    @pl.loop(0, steps)
    def _(k):
        own(k)

    for copy in extras:
        copy.wait()
    prepare(*small, mask, iw, ow, cw)

    @pl.loop(0, steps)
    def _(k):
        @pl.loop(1, levs)
        def _(o):
            part_copy(k, o, me).wait_send()
            part_copy(k, o, peer(o, -1)).wait_recv()


def nt(a, b):
    return lax.dot_general(a, b, (((1,), (1,)), ((), ())), preferred_element_type=F32)


def prepare(cloud_ref, pin_ref, pout_ref, move_ref, iw_ref, ow_ref, cw_ref, mask, iw, ow, cw):
    listed = cloud_ref[...]
    count = listed.shape[1]
    lanes = mask.shape[1]
    high = lax.broadcasted_iota(jnp.int32, (mask.shape[0], count), 0)
    low = lax.broadcasted_iota(jnp.int32, (lanes, count), 0)
    shift = lanes.bit_length() - 1
    hot_high = jnp.where(high == jnp.right_shift(listed, shift), 1.0, 0.0).astype(BF16)
    hot_low = jnp.where(low == jnp.bitwise_and(listed, lanes - 1), 1.0, 0.0).astype(BF16)
    mask[...] = nt(hot_high, hot_low)
    iw[...] = jnp.dot(pin_ref[...], iw_ref[...], preferred_element_type=F32).astype(BF16)
    ow[...] = nt(pout_ref[...], ow_ref[...]).astype(BF16)
    turned = nt(pout_ref[...], cw_ref[...]).astype(BF16)
    cw[: turned.shape[0], :] = nt(turned, pin_ref[...]).astype(BF16)
    cw[turned.shape[0] :, :] = move_ref[...]


def silu(v):
    h = 0.5 * v
    return h * jnp.tanh(h) + h


def physics_kernel(
    rows, lanes, levels, level_pad, layers,
    feat_ref, surf_ref, mask, iw, hw_ref, ow, cw, fields_ref, surface_ref,
):
    step = pl.program_id(0)
    surf = surf_ref[...]
    surf16 = surf.astype(BF16)
    tail = jnp.concatenate([surf16, jnp.zeros_like(surf16)], axis=0)
    feat = jnp.concatenate([feat_ref[r] for r in range(rows)], axis=1)
    feat = jnp.concatenate([feat, tail], axis=0)

    half = rows * lanes // 2
    streams = []
    for s in range(2):
        piece = feat[:, s * half : (s + 1) * half]
        streams.append(
            silu(lax.dot_general(piece, iw[...], (((0,), (0,)), ((), ())), preferred_element_type=F32))
        )
    hid = hw_ref.shape[2]
    cuts = [slice(c, min(c + 256, hid)) for c in range(0, hid, 256)]
    for layer in range(layers):
        for s in range(2):
            operand = streams[s].astype(BF16)
            streams[s] = jnp.concatenate(
                [
                    streams[s][:, cut]
                    + silu(jnp.dot(operand, hw_ref[layer, :, cut], preferred_element_type=F32))
                    for cut in cuts
                ],
                axis=1,
            )
    both = jnp.dot(cw[...], feat, preferred_element_type=F32)
    out_rows = ow.shape[0]
    flat = fields_ref.reshape(levels * 2 * rows, lanes)
    for s in range(2):
        physics = nt(ow[...], streams[s].astype(BF16)).astype(BF16).astype(F32)
        keep = jnp.concatenate(
            [mask[pl.ds(step * rows + s * (rows // 2) + r, 1), :] for r in range(rows // 2)], axis=1
        )
        at = slice(s * half, (s + 1) * half)
        tend = both[:out_rows, at] + jnp.where(keep > 0.5, physics, 0.0)
        tend = tend.astype(BF16).astype(F32)
        for v in range(2):
            first = v * level_pad
            total = (
                both[out_rows + first : out_rows + first + level_pad, at]
                + tend[first : first + level_pad]
            )
            for r in range(rows // 2):
                place = 2 * (s * (rows // 2) + r) + v
                for l in range(0, levels, 8):
                    n = min(8, levels - l)
                    flat[pl.ds(l * 2 * rows + place, n, stride=2 * rows), :] = (
                        total[l : l + n, r * lanes : (r + 1) * lanes]
                    )
        surface_ref[:, at] = surf[:, at] + tend[2 * level_pad : 2 * level_pad + surf.shape[0]]


def orders(levs, lb, lp, levels, level_pad, surf, features):
    size_in = levs * 2 * lp + 2 * surf
    size_out = 2 * level_pad + 2 * surf
    pin = np.zeros((size_in, features), np.float32)
    pout = np.zeros((size_out, features), np.float32)
    for v in range(2):
        for level in range(levels):
            j, l = divmod(level, lb)
            pin[j * 2 * lp + v * lp + l, v * levels + level] = 1.0
            pout[v * level_pad + level, v * levels + level] = 1.0
    for s in range(surf):
        pin[levs * 2 * lp + s, 2 * levels + s] = 1.0
        pout[2 * level_pad + s, 2 * levels + s] = 1.0
    return pin, pout, pout @ pin.T


def local(
    tiles, levs,
    fields, wind_x, wind_y, diffusivity, surface, cloud_list,
    input_weight, hidden_weight, output_weight, clear_weight,
):
    _, lb, nx, ny = fields.shape
    lp = -(-lb // 8) * 8
    levels = lb * levs
    level_pad = -(-levels // 8) * 8
    mine = nx // levs
    group = 2 * lp
    any_spec = pl.BlockSpec(memory_space=pl.ANY)
    vmem_spec = pl.BlockSpec(memory_space=pltpu.VMEM)
    parts = mine // ROWS
    surf, cols = surface.shape
    features, hid = input_weight.shape
    layers = hidden_weight.shape[0]
    orderings = [
        jnp.asarray(m, BF16) for m in orders(levs, lb, lp, levels, level_pad, surf, features)
    ]
    size_out, size_in = orderings[2].shape
    small = [cloud_list.reshape(1, -1), *orderings, input_weight, output_weight, clear_weight]
    feats, mask, iw, ow, cw = pl.pallas_call(
        functools.partial(advect_kernel, tiles, levs, lb, lp, nx, ny),
        out_shape=(
            jax.ShapeDtypeStruct((mine, levs * group, ny), BF16),
            jax.ShapeDtypeStruct((mine, ny), F32),
            jax.ShapeDtypeStruct((size_in, hid), BF16),
            jax.ShapeDtypeStruct((size_out, hid), BF16),
            jax.ShapeDtypeStruct((2 * size_out, size_in), BF16),
        ),
        in_specs=[any_spec] * (4 + len(small)),
        out_specs=(vmem_spec,) * 5,
        scratch_shapes=[pltpu.VMEM(a.shape, a.dtype) for a in small] + [
            pltpu.VMEM(((2 * lb + lp - lb) * nx, ny), F32),
            pltpu.VMEM((3 * lp * nx, ny), F32),
            pltpu.VMEM((nx + 6, group, ny), F32),
            pltpu.VMEM((nx + 4, 5, lp, ny), F32),
            pltpu.VMEM((2, 6, lp, ny), F32),
            pltpu.VMEM((2, 6, lp, ny), F32),
            pltpu.VMEM((levs - 1, mine, group, ny), BF16),
            pltpu.SemaphoreType.DMA((4,)),
            pltpu.SemaphoreType.DMA((len(small),)),
            pltpu.SemaphoreType.DMA((4,)),
            pltpu.SemaphoreType.DMA((4,)),
            pltpu.SemaphoreType.DMA((parts, levs - 1)),
            pltpu.SemaphoreType.DMA((parts, levs - 1)),
        ],
        compiler_params=pltpu.CompilerParams(
            collective_id=0, has_side_effects=True, vmem_limit_bytes=ADVECT_VMEM
        ),
        name="advect",
    )(
        fields.reshape(2 * lb * nx, ny),
        wind_x.reshape(lb * nx, ny),
        wind_y.reshape(lb * nx, ny),
        diffusivity.reshape(lb * nx, ny),
        *small,
    )

    rows = 8
    wide = rows * ny
    fields_out, surface_out = pl.pallas_call(
        functools.partial(physics_kernel, rows, ny, levels, level_pad, layers),
        grid=(mine // rows,),
        out_shape=(
            jax.ShapeDtypeStruct((levels, mine * 2, ny), F32),
            jax.ShapeDtypeStruct((surf, cols), F32),
        ),
        in_specs=[
            pl.BlockSpec((rows, levs * group, ny), lambda i: (i, 0, 0)),
            pl.BlockSpec((surf, wide), lambda i: (0, i)),
        ] + [vmem_spec] * 5,
        out_specs=(
            pl.BlockSpec((levels, 2 * rows, ny), lambda i: (0, i, 0)),
            pl.BlockSpec((surf, wide), lambda i: (0, i)),
        ),
        compiler_params=pltpu.CompilerParams(vmem_limit_bytes=PHYSICS_VMEM),
        name="physics",
    )(feats, surface, mask, iw, hidden_weight, ow, cw)
    fields_out = fields_out.reshape(levels, mine, 2, ny).transpose(2, 0, 1, 3)
    return fields_out.reshape(2, levels, cols), surface_out


def solution(mesh):
    return jax.shard_map(
        functools.partial(local, mesh.shape["tile"], mesh.shape["lev"]),
        mesh=mesh,
        in_specs=(
            P(None, "lev", "tile", None),
            P("lev", "tile", None),
            P("lev", "tile", None),
            P("lev", "tile", None),
            P(None, ("tile", "lev")),
            P(("tile", "lev")),
            P(),
            P(),
            P(),
            P(),
        ),
        out_specs=(P(None, None, ("tile", "lev")), P(None, ("tile", "lev"))),
        check_vma=False,
    )
```

```python
import functools

import numpy as np
import jax
import jax.numpy as jnp
from jax import lax
from jax.experimental import pallas as pl
from jax.experimental.pallas import tpu as pltpu
from jax.sharding import PartitionSpec as P

F32 = jnp.float32
BF16 = jnp.bfloat16
ROWS = 8
ADVECT_VMEM = 58 * 1024 * 1024
PHYSICS_VMEM = 58 * 1024 * 1024


def advect_kernel(
    tiles, levs, lb, lp, nx, ny, levels, level_pad,
    f_hbm, wx_hbm, wy_hbm, d_hbm, *refs,
):
    small_hbm, refs = refs[:9], refs[9:]
    out_ref, mask, iw, ow, cw, fields_ref, surface_ref = refs[:7]
    small, refs = refs[7:16], refs[16:]
    fv, wv, padded, coef, edge_out, edge_in, outbox, load_sem, small_sem = refs[:9]
    halo_send, halo_recv, part_send, part_recv = refs[9:]
    tile = lax.axis_index("tile")
    me = lax.axis_index("lev")
    right = lax.rem(tile + 1, tiles)
    left = lax.rem(tile + tiles - 1, tiles)
    mine = nx // levs
    steps = mine // ROWS
    group = 2 * lp

    loads = [pltpu.make_async_copy(f_hbm, fv.at[pl.ds(0, 2 * lb * nx)], load_sem.at[0])]
    for i, ref in enumerate((wx_hbm, wy_hbm, d_hbm)):
        loads.append(
            pltpu.make_async_copy(ref, wv.at[pl.ds(i * lp * nx, lb * nx)], load_sem.at[i + 1])
        )
    extras = [
        pltpu.make_async_copy(src, dst, small_sem.at[i])
        for i, (src, dst) in enumerate(zip(small_hbm, small))
    ]
    for copy in loads + extras:
        copy.start()

    barrier = pltpu.get_barrier_semaphore()
    for near in (left, right):
        pl.semaphore_signal(
            barrier, inc=1, device_id={"tile": near}, device_id_type=pl.DeviceIdType.MESH
        )
    for o in range(1, levs):
        pl.semaphore_signal(
            barrier, inc=1, device_id={"lev": lax.rem(me + o, levs)},
            device_id_type=pl.DeviceIdType.MESH,
        )

    extra = lp - lb
    if extra:
        fv[pl.ds(2 * lb * nx, extra * nx), :] = jnp.zeros((extra * nx, ny), F32)
        for i in range(3):
            wv[pl.ds((i * lp + lb) * nx, extra * nx), :] = jnp.zeros((extra * nx, ny), F32)

    lane = lax.broadcasted_iota(jnp.int32, (lp, ny), 1)
    north_ok = lane < ny - 1
    south_ok = lane > 0

    def level_rows(ref, first, x):
        parts = [ref[pl.ds((first + 8 * h) * nx + x, 8, stride=nx), :] for h in range(lp // 8)]
        return jnp.concatenate(parts, axis=0)

    def convert(x):
        for v in range(2):
            padded[x + 3, v * lp : (v + 1) * lp, :] = level_rows(fv, v * lb, x)

    def set_coef(row, wx, wy, d):
        wx = 0.5 * wx
        wy = 0.5 * wy
        coef[row, 0] = d - wx
        coef[row, 1] = d + wx
        coef[row, 2] = jnp.where(north_ok, d - wy, 0.0)
        coef[row, 3] = jnp.where(south_ok, d + wy, 0.0)
        coef[row, 4] = 4.0 * d

    for copy in loads:
        copy.wait()
    for x in (0, 1, 2, nx - 3, nx - 2, nx - 1):
        convert(x)
    for side, first in ((0, 0), (1, nx - 2)):
        for r in range(2):
            for i in range(3):
                edge_out[side, r * 3 + i] = level_rows(wv, i * lp, first + r)

    pl.semaphore_wait(barrier, 2 + levs - 1)

    def halo_copy(src, dst, index, near):
        return pltpu.make_async_remote_copy(
            src_ref=src, dst_ref=dst, send_sem=halo_send.at[index], recv_sem=halo_recv.at[index],
            device_id={"tile": near}, device_id_type=pl.DeviceIdType.MESH,
        )

    halos = [
        halo_copy(padded.at[pl.ds(nx, 3)], padded.at[pl.ds(0, 3)], 0, right),
        halo_copy(padded.at[pl.ds(3, 3)], padded.at[pl.ds(nx + 3, 3)], 1, left),
        halo_copy(edge_out.at[1], edge_in.at[0], 2, right),
        halo_copy(edge_out.at[0], edge_in.at[1], 3, left),
    ]
    for copy in halos:
        copy.start()

    @pl.loop(0, nx // 8)
    def _(b):
        for r in range(8):
            x = b * 8 + r
            set_coef(x + 2, *(level_rows(wv, i * lp, x) for i in range(3)))

    @pl.loop(0, (nx - 6) // 2, unroll=4)
    def _(b):
        for r in range(2):
            convert(3 + b * 2 + r)

    def rate(c, e, w, row):
        north = pltpu.roll(c, ny - 1, axis=1)
        south = pltpu.roll(c, 1, axis=1)
        return (
            coef[row, 0] * e + coef[row, 1] * w + coef[row, 2] * north + coef[row, 3] * south
            - coef[row, 4] * c
        )

    def section(x0, save):
        for v in range(2):
            lo, hi = v * lp, (v + 1) * lp
            f = [padded[x0 + i, lo:hi, :] for i in range(2)]
            one = []
            two = []
            for r in range(ROWS + 4):
                f.append(padded[x0 + r + 2, lo:hi, :])
                one.append(f[r + 1] + rate(f[r + 1], f[r + 2], f[r], x0 + r) * (1.0 / 3.0))
                if r >= 2:
                    two.append(
                        f[r] + 0.5 * rate(one[r - 1], one[r], one[r - 2], x0 + r - 1)
                    )
                if r >= 4:
                    done = f[r - 1] + rate(two[r - 3], two[r - 2], two[r - 4], x0 + r - 2)
                    save(r - 4, lo, done.astype(BF16))

    pair = 2 if levs % 2 == 0 else 1
    chips = levs // pair
    high, low = me // pair, lax.rem(me, pair)

    def peer(o, sign):
        far = lax.rem(high + (o // pair if sign > 0 else chips - o // pair), chips)
        return far * pair + lax.rem(low + (o % pair if sign > 0 else pair - o % pair), pair)

    def part_copy(k, o, source):
        return pltpu.make_async_remote_copy(
            src_ref=outbox.at[o - 1, pl.ds(k * ROWS, ROWS)],
            dst_ref=out_ref.at[pl.ds(k * ROWS, ROWS), pl.ds(pl.multiple_of(source * group, group), group)],
            send_sem=part_send.at[k, o - 1],
            recv_sem=part_recv.at[k, o - 1],
            device_id={"lev": peer(o, 1)},
            device_id_type=pl.DeviceIdType.MESH,
        )

    def step(k, o):
        def save(r, lo, value):
            outbox[o - 1, k * ROWS + r, lo : lo + lp, :] = value

        section(peer(o, 1) * mine + k * ROWS, save)
        part_copy(k, o, me).start()

    def own(k):
        base = pl.multiple_of(me * group, group)

        def save(r, lo, value):
            out_ref[k * ROWS + r, pl.ds(base + lo, lp), :] = value

        section(me * mine + k * ROWS, save)

    def batch(first, stride, count):
        @pl.loop(0, count)
        def _(i):
            @pl.loop(pair, levs)
            def _(o):
                step(first + i * stride, o)

        @pl.loop(0, count)
        def _(i):
            @pl.loop(1, pair)
            def _(o):
                step(first + i * stride, o)

        @pl.loop(0, count)
        def _(i):
            own(first + i * stride)

    batch(1, 1, steps - 2)

    for copy in halos:
        copy.wait()
    for side, first in ((0, 0), (1, nx + 2)):
        for r in range(2):
            set_coef(first + r, *(edge_in[side, r * 3 + i] for i in range(3)))

    batch(0, steps - 1, 2)

    for copy in extras:
        copy.wait()
    prepare(*small[:7], mask, iw, ow, cw)
    hidden, surf_ref = small[7:]

    def finish(k):
        @pl.loop(1, levs)
        def _(o):
            part_copy(k, o, me).wait_send()
            part_copy(k, o, peer(o, -1)).wait_recv()

    flat = fields_ref.reshape(levels * 2 * ROWS * (steps - 2), ny)
    wide = ROWS * ny

    @pl.loop(1, steps - 1)
    def _(k):
        finish(k)
        at = pl.ds(pl.multiple_of((k - 1) * wide, wide), wide)
        surface_ref[:, at] = column_physics(
            [out_ref[k * ROWS + r] for r in range(ROWS)],
            [mask[pl.ds(k * ROWS + r, 1), :] for r in range(ROWS)],
            surf_ref[:, pl.ds(pl.multiple_of(k * wide, wide), wide)],
            iw, hidden, ow, cw, levels, level_pad,
            flat, 2 * ROWS * (k - 1), 2 * ROWS * (steps - 2),
        )

    @pl.loop(0, 2)
    def _(i):
        finish(i * (steps - 1))


def nt(a, b):
    return lax.dot_general(a, b, (((1,), (1,)), ((), ())), preferred_element_type=F32)


def prepare(cloud_ref, pin_ref, pout_ref, move_ref, iw_ref, ow_ref, cw_ref, mask, iw, ow, cw):
    listed = cloud_ref[...]
    count = listed.shape[1]
    lanes = mask.shape[1]
    high = lax.broadcasted_iota(jnp.int32, (mask.shape[0], count), 0)
    low = lax.broadcasted_iota(jnp.int32, (lanes, count), 0)
    shift = lanes.bit_length() - 1
    hot_high = jnp.where(high == jnp.right_shift(listed, shift), 1.0, 0.0).astype(BF16)
    hot_low = jnp.where(low == jnp.bitwise_and(listed, lanes - 1), 1.0, 0.0).astype(BF16)
    mask[...] = nt(hot_high, hot_low)
    iw[...] = jnp.dot(pin_ref[...], iw_ref[...], preferred_element_type=F32).astype(BF16)
    ow[...] = nt(pout_ref[...], ow_ref[...]).astype(BF16)
    turned = nt(pout_ref[...], cw_ref[...]).astype(BF16)
    cw[: turned.shape[0], :] = nt(turned, pin_ref[...]).astype(BF16)
    cw[turned.shape[0] :, :] = move_ref[...]


def silu(v):
    h = 0.5 * v
    return h * jnp.tanh(h) + h


def column_physics(
    feat, masks, surf, iw, hidden, ow, cw, levels, level_pad, flat, place, stride
):
    rows, lanes = len(feat), feat[0].shape[1]
    surf16 = surf.astype(BF16)
    tail = jnp.concatenate([surf16, jnp.zeros_like(surf16)], axis=0)
    feat = jnp.concatenate([jnp.concatenate(feat, axis=1), tail], axis=0)

    per = rows // 2
    half = per * lanes
    streams = []
    for s in range(2):
        piece = feat[:, s * half : (s + 1) * half]
        streams.append(
            silu(lax.dot_general(piece, iw[...], (((0,), (0,)), ((), ())), preferred_element_type=F32))
        )
    layers, _, hid = hidden.shape
    cuts = [slice(c, min(c + 256, hid)) for c in range(0, hid, 256)]
    for layer in range(layers):
        for s in range(2):
            operand = streams[s].astype(BF16)
            streams[s] = jnp.concatenate(
                [
                    streams[s][:, cut]
                    + silu(jnp.dot(operand, hidden[layer, :, cut], preferred_element_type=F32))
                    for cut in cuts
                ],
                axis=1,
            )
    both = jnp.dot(cw[...], feat, preferred_element_type=F32)
    out_rows = ow.shape[0]
    surfaces = []
    for s in range(2):
        physics = nt(ow[...], streams[s].astype(BF16)).astype(BF16).astype(F32)
        keep = jnp.concatenate(masks[s * per : (s + 1) * per], axis=1)
        at = slice(s * half, (s + 1) * half)
        tend = both[:out_rows, at] + jnp.where(keep > 0.5, physics, 0.0)
        tend = tend.astype(BF16).astype(F32)
        for v in range(2):
            first = v * level_pad
            total = (
                both[out_rows + first : out_rows + first + level_pad, at]
                + tend[first : first + level_pad]
            )
            for r in range(per):
                for l in range(0, levels, 8):
                    n = min(8, levels - l)
                    start = l * stride + place + 2 * (s * per + r) + v
                    flat[pl.ds(start, n, stride=stride), :] = (
                        total[l : l + n, r * lanes : (r + 1) * lanes]
                    )
        surfaces.append(surf[:, at] + tend[2 * level_pad : 2 * level_pad + surf.shape[0]])
    return jnp.concatenate(surfaces, axis=1)


def physics_kernel(
    steps, lanes, levels, level_pad,
    feat_ref, surf_ref, part_ref, surf_part_ref, mask, iw, hidden, ow, cw,
    fields_ref, surface_ref,
):
    step = pl.program_id(0)
    inner = jnp.logical_and(step > 0, step < steps - 1)

    @pl.when(inner)
    def _():
        fields_ref[...] = part_ref[...]
        surface_ref[...] = surf_part_ref[...]

    @pl.when(jnp.logical_not(inner))
    def _():
        flat = fields_ref.reshape(levels * 2 * ROWS, lanes)
        surface_ref[...] = column_physics(
            [feat_ref[r] for r in range(ROWS)],
            [mask[pl.ds(step * ROWS + r, 1), :] for r in range(ROWS)],
            surf_ref[...], iw, hidden, ow, cw, levels, level_pad, flat, 0, 2 * ROWS,
        )


def orders(levs, lb, lp, levels, level_pad, surf, features):
    size_in = levs * 2 * lp + 2 * surf
    size_out = 2 * level_pad + 2 * surf
    pin = np.zeros((size_in, features), np.float32)
    pout = np.zeros((size_out, features), np.float32)
    for v in range(2):
        for level in range(levels):
            j, l = divmod(level, lb)
            pin[j * 2 * lp + v * lp + l, v * levels + level] = 1.0
            pout[v * level_pad + level, v * levels + level] = 1.0
    for s in range(surf):
        pin[levs * 2 * lp + s, 2 * levels + s] = 1.0
        pout[2 * level_pad + s, 2 * levels + s] = 1.0
    return pin, pout, pout @ pin.T


def local(
    tiles, levs,
    fields, wind_x, wind_y, diffusivity, surface, cloud_list,
    input_weight, hidden_weight, output_weight, clear_weight,
):
    _, lb, nx, ny = fields.shape
    lp = -(-lb // 8) * 8
    levels = lb * levs
    level_pad = -(-levels // 8) * 8
    mine = nx // levs
    group = 2 * lp
    any_spec = pl.BlockSpec(memory_space=pl.ANY)
    vmem_spec = pl.BlockSpec(memory_space=pltpu.VMEM)
    parts = mine // ROWS
    surf, cols = surface.shape
    features, hid = input_weight.shape
    orderings = [
        jnp.asarray(m, BF16) for m in orders(levs, lb, lp, levels, level_pad, surf, features)
    ]
    size_out, size_in = orderings[2].shape
    small = [cloud_list.reshape(1, -1), *orderings, input_weight, output_weight, clear_weight]
    small += [hidden_weight, surface]
    feats, mask, iw, ow, cw, part, surf_part = pl.pallas_call(
        functools.partial(advect_kernel, tiles, levs, lb, lp, nx, ny, levels, level_pad),
        out_shape=(
            jax.ShapeDtypeStruct((mine, levs * group, ny), BF16),
            jax.ShapeDtypeStruct((mine, ny), F32),
            jax.ShapeDtypeStruct((size_in, hid), BF16),
            jax.ShapeDtypeStruct((size_out, hid), BF16),
            jax.ShapeDtypeStruct((2 * size_out, size_in), BF16),
            jax.ShapeDtypeStruct((levels, 2 * ROWS * (parts - 2), ny), F32),
            jax.ShapeDtypeStruct((surf, ROWS * (parts - 2) * ny), F32),
        ),
        in_specs=[any_spec] * (4 + len(small)),
        out_specs=(vmem_spec,) * 7,
        scratch_shapes=[pltpu.VMEM(a.shape, a.dtype) for a in small] + [
            pltpu.VMEM(((2 * lb + lp - lb) * nx, ny), F32),
            pltpu.VMEM((3 * lp * nx, ny), F32),
            pltpu.VMEM((nx + 6, group, ny), F32),
            pltpu.VMEM((nx + 4, 5, lp, ny), F32),
            pltpu.VMEM((2, 6, lp, ny), F32),
            pltpu.VMEM((2, 6, lp, ny), F32),
            pltpu.VMEM((levs - 1, mine, group, ny), BF16),
            pltpu.SemaphoreType.DMA((4,)),
            pltpu.SemaphoreType.DMA((len(small),)),
            pltpu.SemaphoreType.DMA((4,)),
            pltpu.SemaphoreType.DMA((4,)),
            pltpu.SemaphoreType.DMA((parts, levs - 1)),
            pltpu.SemaphoreType.DMA((parts, levs - 1)),
        ],
        compiler_params=pltpu.CompilerParams(
            collective_id=0, has_side_effects=True, vmem_limit_bytes=ADVECT_VMEM
        ),
        name="advect",
    )(
        fields.reshape(2 * lb * nx, ny),
        wind_x.reshape(lb * nx, ny),
        wind_y.reshape(lb * nx, ny),
        diffusivity.reshape(lb * nx, ny),
        *small,
    )

    wide = ROWS * ny

    def inner(i):
        return jnp.clip(i - 1, 0, parts - 3)

    fields_out, surface_out = pl.pallas_call(
        functools.partial(physics_kernel, parts, ny, levels, level_pad),
        grid=(parts,),
        out_shape=(
            jax.ShapeDtypeStruct((levels, mine * 2, ny), F32),
            jax.ShapeDtypeStruct((surf, cols), F32),
        ),
        in_specs=[
            pl.BlockSpec((ROWS, levs * group, ny), lambda i: (i, 0, 0)),
            pl.BlockSpec((surf, wide), lambda i: (0, i)),
            pl.BlockSpec((levels, 2 * ROWS, ny), lambda i: (0, inner(i), 0)),
            pl.BlockSpec((surf, wide), lambda i: (0, inner(i))),
        ] + [vmem_spec] * 5,
        out_specs=(
            pl.BlockSpec((levels, 2 * ROWS, ny), lambda i: (0, i, 0)),
            pl.BlockSpec((surf, wide), lambda i: (0, i)),
        ),
        compiler_params=pltpu.CompilerParams(vmem_limit_bytes=PHYSICS_VMEM),
        name="physics",
    )(feats, surface, part, surf_part, mask, iw, hidden_weight, ow, cw)
    fields_out = fields_out.reshape(levels, mine, 2, ny).transpose(2, 0, 1, 3)
    return fields_out.reshape(2, levels, cols), surface_out


def solution(mesh):
    return jax.shard_map(
        functools.partial(local, mesh.shape["tile"], mesh.shape["lev"]),
        mesh=mesh,
        in_specs=(
            P(None, "lev", "tile", None),
            P("lev", "tile", None),
            P("lev", "tile", None),
            P("lev", "tile", None),
            P(None, ("tile", "lev")),
            P(("tile", "lev")),
            P(),
            P(),
            P(),
            P(),
        ),
        out_specs=(P(None, None, ("tile", "lev")), P(None, ("tile", "lev"))),
        check_vma=False,
    )
```

```python
import functools

import numpy as np
import jax
import jax.numpy as jnp
from jax import lax
from jax.experimental import pallas as pl
from jax.experimental.pallas import tpu as pltpu
from jax.sharding import PartitionSpec as P

F32 = jnp.float32
BF16 = jnp.bfloat16
ROWS = 8
ADVECT_VMEM = 58 * 1024 * 1024


def advect_kernel(
    tiles, levs, lb, lp, nx, ny, levels, level_pad,
    f_hbm, wx_hbm, wy_hbm, d_hbm, *refs,
):
    small_hbm, refs = refs[:9], refs[9:]
    fields_hbm, surface_ref = refs[:2]
    out_ref, mask, iw, ow, cw, flat, out_sem = refs[2:9]
    small, refs = refs[9:18], refs[18:]
    fv, wv, padded, coef, edge_out, edge_in, outbox, load_sem, small_sem = refs[:9]
    halo_send, halo_recv, part_send, part_recv = refs[9:]
    tile = lax.axis_index("tile")
    me = lax.axis_index("lev")
    right = lax.rem(tile + 1, tiles)
    left = lax.rem(tile + tiles - 1, tiles)
    mine = nx // levs
    steps = mine // ROWS
    group = 2 * lp

    loads = [pltpu.make_async_copy(f_hbm, fv.at[pl.ds(0, 2 * lb * nx)], load_sem.at[0])]
    for i, ref in enumerate((wx_hbm, wy_hbm, d_hbm)):
        loads.append(
            pltpu.make_async_copy(ref, wv.at[pl.ds(i * lp * nx, lb * nx)], load_sem.at[i + 1])
        )
    extras = [
        pltpu.make_async_copy(src, dst, small_sem.at[i])
        for i, (src, dst) in enumerate(zip(small_hbm, small))
    ]
    for copy in loads + extras:
        copy.start()

    barrier = pltpu.get_barrier_semaphore()
    for near in (left, right):
        pl.semaphore_signal(
            barrier, inc=1, device_id={"tile": near}, device_id_type=pl.DeviceIdType.MESH
        )
    for o in range(1, levs):
        pl.semaphore_signal(
            barrier, inc=1, device_id={"lev": lax.rem(me + o, levs)},
            device_id_type=pl.DeviceIdType.MESH,
        )

    extra = lp - lb
    if extra:
        fv[pl.ds(2 * lb * nx, extra * nx), :] = jnp.zeros((extra * nx, ny), F32)
        for i in range(3):
            wv[pl.ds((i * lp + lb) * nx, extra * nx), :] = jnp.zeros((extra * nx, ny), F32)

    lane = lax.broadcasted_iota(jnp.int32, (lp, ny), 1)
    north_ok = lane < ny - 1
    south_ok = lane > 0

    def level_rows(ref, first, x):
        parts = [ref[pl.ds((first + 8 * h) * nx + x, 8, stride=nx), :] for h in range(lp // 8)]
        return jnp.concatenate(parts, axis=0)

    def convert(x):
        for v in range(2):
            padded[x + 3, v * lp : (v + 1) * lp, :] = level_rows(fv, v * lb, x)

    def set_coef(row, wx, wy, d):
        wx = 0.5 * wx
        wy = 0.5 * wy
        coef[row, 0] = d - wx
        coef[row, 1] = d + wx
        coef[row, 2] = jnp.where(north_ok, d - wy, 0.0)
        coef[row, 3] = jnp.where(south_ok, d + wy, 0.0)
        coef[row, 4] = 4.0 * d

    for copy in loads:
        copy.wait()
    for x in (0, 1, 2, nx - 3, nx - 2, nx - 1):
        convert(x)
    for side, first in ((0, 0), (1, nx - 2)):
        for r in range(2):
            for i in range(3):
                edge_out[side, r * 3 + i] = level_rows(wv, i * lp, first + r)

    pl.semaphore_wait(barrier, 2 + levs - 1)

    def halo_copy(src, dst, index, near):
        return pltpu.make_async_remote_copy(
            src_ref=src, dst_ref=dst, send_sem=halo_send.at[index], recv_sem=halo_recv.at[index],
            device_id={"tile": near}, device_id_type=pl.DeviceIdType.MESH,
        )

    halos = [
        halo_copy(padded.at[pl.ds(nx, 3)], padded.at[pl.ds(0, 3)], 0, right),
        halo_copy(padded.at[pl.ds(3, 3)], padded.at[pl.ds(nx + 3, 3)], 1, left),
        halo_copy(edge_out.at[1], edge_in.at[0], 2, right),
        halo_copy(edge_out.at[0], edge_in.at[1], 3, left),
    ]
    for copy in halos:
        copy.start()

    @pl.loop(0, nx // 8)
    def _(b):
        for r in range(8):
            x = b * 8 + r
            set_coef(x + 2, *(level_rows(wv, i * lp, x) for i in range(3)))

    @pl.loop(0, (nx - 6) // 2, unroll=4)
    def _(b):
        for r in range(2):
            convert(3 + b * 2 + r)

    def rate(c, e, w, weights):
        north = pltpu.roll(c, ny - 1, axis=1)
        south = pltpu.roll(c, 1, axis=1)
        return (
            weights[0] * e + weights[1] * w + weights[2] * north + weights[3] * south
            - weights[4] * c
        )

    def section(x0, save):
        cuts = [slice(v * lp, (v + 1) * lp) for v in range(2)]
        f = [[padded[x0 + i, cut, :] for i in range(2)] for cut in cuts]
        one = [[], []]
        two = [[], []]
        for r in range(ROWS + 4):
            weights = [coef[x0 + r, i] for i in range(5)]
            for v in range(2):
                g = f[v]
                g.append(padded[x0 + r + 2, cuts[v], :])
                one[v].append(g[r + 1] + rate(g[r + 1], g[r + 2], g[r], weights) * (1.0 / 3.0))
            if r >= 2:
                weights = [coef[x0 + r - 1, i] for i in range(5)]
                for v in range(2):
                    o = one[v]
                    two[v].append(f[v][r] + 0.5 * rate(o[r - 1], o[r], o[r - 2], weights))
            if r >= 4:
                weights = [coef[x0 + r - 2, i] for i in range(5)]
                for v in range(2):
                    t = two[v]
                    done = f[v][r - 1] + rate(t[r - 3], t[r - 2], t[r - 4], weights)
                    save(r - 4, v * lp, done.astype(BF16))

    pair = 2 if levs % 2 == 0 else 1
    chips = levs // pair
    high, low = me // pair, lax.rem(me, pair)

    def peer(o, sign):
        far = lax.rem(high + (o // pair if sign > 0 else chips - o // pair), chips)
        return far * pair + lax.rem(low + (o % pair if sign > 0 else pair - o % pair), pair)

    def part_copy(k, o, source):
        return pltpu.make_async_remote_copy(
            src_ref=outbox.at[o - 1, pl.ds(k * ROWS, ROWS)],
            dst_ref=out_ref.at[pl.ds(k * ROWS, ROWS), pl.ds(pl.multiple_of(source * group, group), group)],
            send_sem=part_send.at[k, o - 1],
            recv_sem=part_recv.at[k, o - 1],
            device_id={"lev": peer(o, 1)},
            device_id_type=pl.DeviceIdType.MESH,
        )

    def step(k, o):
        def save(r, lo, value):
            outbox[o - 1, k * ROWS + r, lo : lo + lp, :] = value

        section(peer(o, 1) * mine + k * ROWS, save)
        part_copy(k, o, me).start()

    def own(k):
        base = pl.multiple_of(me * group, group)

        def save(r, lo, value):
            out_ref[k * ROWS + r, pl.ds(base + lo, lp), :] = value

        section(me * mine + k * ROWS, save)

    def batch(first, stride, count):
        @pl.loop(0, count)
        def _(i):
            @pl.loop(pair, levs)
            def _(o):
                step(first + i * stride, o)

        @pl.loop(0, count)
        def _(i):
            @pl.loop(1, pair)
            def _(o):
                step(first + i * stride, o)

        @pl.loop(0, count)
        def _(i):
            own(first + i * stride)

    batch(1, 1, steps - 2)

    for copy in halos:
        copy.wait()
    for side, first in ((0, 0), (1, nx + 2)):
        for r in range(2):
            set_coef(first + r, *(edge_in[side, r * 3 + i] for i in range(3)))

    batch(0, steps - 1, 2)

    for copy in extras:
        copy.wait()
    prepare(*small[:7], mask, iw, ow, cw)
    hidden, surf_ref = small[7:]

    def finish(k):
        @pl.loop(1, levs)
        def _(o):
            part_copy(k, o, me).wait_send()
            part_copy(k, o, peer(o, -1)).wait_recv()

    wide = ROWS * ny
    blocks = flat.reshape(levels, 2 * mine, ny)

    def write(k):
        at = pl.ds(pl.multiple_of(k * 2 * ROWS, 2 * ROWS), 2 * ROWS)
        return pltpu.make_async_copy(
            blocks.at[:, at, :], fields_hbm.at[:, at, :], out_sem.at[k]
        )

    def columns(k):
        finish(k)
        at = pl.ds(pl.multiple_of(k * wide, wide), wide)
        surface_ref[:, at] = column_physics(
            [out_ref[k * ROWS + r] for r in range(ROWS)],
            [mask[pl.ds(k * ROWS + r, 1), :] for r in range(ROWS)],
            surf_ref[:, at], iw, hidden, ow, cw, levels, level_pad,
            flat, 2 * ROWS * k, 2 * mine,
        )
        write(k).start()

    @pl.loop(0, steps)
    def _(i):
        columns(lax.rem(i + 1, steps - 1) + (i // (steps - 1)) * (steps - 2))

    @pl.loop(0, steps)
    def _(k):
        write(k).wait()


def nt(a, b):
    return lax.dot_general(a, b, (((1,), (1,)), ((), ())), preferred_element_type=F32)


def prepare(cloud_ref, pin_ref, pout_ref, move_ref, iw_ref, ow_ref, cw_ref, mask, iw, ow, cw):
    listed = cloud_ref[...]
    count = listed.shape[1]
    lanes = mask.shape[1]
    high = lax.broadcasted_iota(jnp.int32, (mask.shape[0], count), 0)
    low = lax.broadcasted_iota(jnp.int32, (lanes, count), 0)
    shift = lanes.bit_length() - 1
    hot_high = jnp.where(high == jnp.right_shift(listed, shift), 1.0, 0.0).astype(BF16)
    hot_low = jnp.where(low == jnp.bitwise_and(listed, lanes - 1), 1.0, 0.0).astype(BF16)
    mask[...] = nt(hot_high, hot_low)
    iw[...] = jnp.dot(pin_ref[...], iw_ref[...], preferred_element_type=F32).astype(BF16)
    ow[...] = nt(pout_ref[...], ow_ref[...]).astype(BF16)
    turned = nt(pout_ref[...], cw_ref[...]).astype(BF16)
    cw[: turned.shape[0], :] = nt(turned, pin_ref[...]).astype(BF16)
    cw[turned.shape[0] :, :] = move_ref[...]


def silu(v):
    h = 0.5 * v
    return h * jnp.tanh(h) + h


def column_physics(
    feat, masks, surf, iw, hidden, ow, cw, levels, level_pad, flat, place, stride
):
    rows, lanes = len(feat), feat[0].shape[1]
    surf16 = surf.astype(BF16)
    tail = jnp.concatenate([surf16, jnp.zeros_like(surf16)], axis=0)
    feat = jnp.concatenate([jnp.concatenate(feat, axis=1), tail], axis=0)

    per = rows // 2
    half = per * lanes
    streams = []
    for s in range(2):
        piece = feat[:, s * half : (s + 1) * half]
        streams.append(
            silu(lax.dot_general(piece, iw[...], (((0,), (0,)), ((), ())), preferred_element_type=F32))
        )
    layers, _, hid = hidden.shape
    cuts = [slice(c, min(c + 256, hid)) for c in range(0, hid, 256)]
    for layer in range(layers):
        for s in range(2):
            operand = streams[s].astype(BF16)
            streams[s] = jnp.concatenate(
                [
                    streams[s][:, cut]
                    + silu(jnp.dot(operand, hidden[layer, :, cut], preferred_element_type=F32))
                    for cut in cuts
                ],
                axis=1,
            )
    both = jnp.dot(cw[...], feat, preferred_element_type=F32)
    out_rows = ow.shape[0]
    surfaces = []
    for s in range(2):
        physics = nt(ow[...], streams[s].astype(BF16)).astype(BF16).astype(F32)
        keep = jnp.concatenate(masks[s * per : (s + 1) * per], axis=1)
        at = slice(s * half, (s + 1) * half)
        tend = both[:out_rows, at] + jnp.where(keep > 0.5, physics, 0.0)
        tend = tend.astype(BF16).astype(F32)
        for v in range(2):
            first = v * level_pad
            total = (
                both[out_rows + first : out_rows + first + level_pad, at]
                + tend[first : first + level_pad]
            )
            for r in range(per):
                for l in range(0, levels, 8):
                    n = min(8, levels - l)
                    start = l * stride + place + 2 * (s * per + r) + v
                    flat[pl.ds(start, n, stride=stride), :] = (
                        total[l : l + n, r * lanes : (r + 1) * lanes]
                    )
        surfaces.append(surf[:, at] + tend[2 * level_pad : 2 * level_pad + surf.shape[0]])
    return jnp.concatenate(surfaces, axis=1)


def orders(levs, lb, lp, levels, level_pad, surf, features):
    size_in = levs * 2 * lp + 2 * surf
    size_out = 2 * level_pad + 2 * surf
    pin = np.zeros((size_in, features), np.float32)
    pout = np.zeros((size_out, features), np.float32)
    for v in range(2):
        for level in range(levels):
            j, l = divmod(level, lb)
            pin[j * 2 * lp + v * lp + l, v * levels + level] = 1.0
            pout[v * level_pad + level, v * levels + level] = 1.0
    for s in range(surf):
        pin[levs * 2 * lp + s, 2 * levels + s] = 1.0
        pout[2 * level_pad + s, 2 * levels + s] = 1.0
    return pin, pout, pout @ pin.T


def local(
    tiles, levs,
    fields, wind_x, wind_y, diffusivity, surface, cloud_list,
    input_weight, hidden_weight, output_weight, clear_weight,
):
    _, lb, nx, ny = fields.shape
    lp = -(-lb // 8) * 8
    levels = lb * levs
    level_pad = -(-levels // 8) * 8
    mine = nx // levs
    group = 2 * lp
    any_spec = pl.BlockSpec(memory_space=pl.ANY)
    vmem_spec = pl.BlockSpec(memory_space=pltpu.VMEM)
    parts = mine // ROWS
    surf, cols = surface.shape
    features, hid = input_weight.shape
    orderings = [
        jnp.asarray(m, BF16) for m in orders(levs, lb, lp, levels, level_pad, surf, features)
    ]
    size_out, size_in = orderings[2].shape
    small = [cloud_list.reshape(1, -1), *orderings, input_weight, output_weight, clear_weight]
    small += [hidden_weight, surface]
    fields_out, surface_out = pl.pallas_call(
        functools.partial(advect_kernel, tiles, levs, lb, lp, nx, ny, levels, level_pad),
        out_shape=(
            jax.ShapeDtypeStruct((levels, mine * 2, ny), F32),
            jax.ShapeDtypeStruct((surf, cols), F32),
        ),
        in_specs=[any_spec] * (4 + len(small)),
        out_specs=(any_spec, vmem_spec),
        scratch_shapes=[
            pltpu.VMEM((mine, levs * group, ny), BF16),
            pltpu.VMEM((mine, ny), F32),
            pltpu.VMEM((size_in, hid), BF16),
            pltpu.VMEM((size_out, hid), BF16),
            pltpu.VMEM((2 * size_out, size_in), BF16),
            pltpu.VMEM((levels * mine * 2, ny), F32),
            pltpu.SemaphoreType.DMA((parts,)),
        ] + [pltpu.VMEM(a.shape, a.dtype) for a in small] + [
            pltpu.VMEM(((2 * lb + lp - lb) * nx, ny), F32),
            pltpu.VMEM((3 * lp * nx, ny), F32),
            pltpu.VMEM((nx + 6, group, ny), F32),
            pltpu.VMEM((nx + 4, 5, lp, ny), F32),
            pltpu.VMEM((2, 6, lp, ny), F32),
            pltpu.VMEM((2, 6, lp, ny), F32),
            pltpu.VMEM((levs - 1, mine, group, ny), BF16),
            pltpu.SemaphoreType.DMA((4,)),
            pltpu.SemaphoreType.DMA((len(small),)),
            pltpu.SemaphoreType.DMA((4,)),
            pltpu.SemaphoreType.DMA((4,)),
            pltpu.SemaphoreType.DMA((parts, levs - 1)),
            pltpu.SemaphoreType.DMA((parts, levs - 1)),
        ],
        compiler_params=pltpu.CompilerParams(
            collective_id=0, has_side_effects=True, vmem_limit_bytes=ADVECT_VMEM
        ),
        name="advect",
    )(
        fields.reshape(2 * lb * nx, ny),
        wind_x.reshape(lb * nx, ny),
        wind_y.reshape(lb * nx, ny),
        diffusivity.reshape(lb * nx, ny),
        *small,
    )

    fields_out = fields_out.reshape(levels, mine, 2, ny).transpose(2, 0, 1, 3)
    return fields_out.reshape(2, levels, cols), surface_out


def solution(mesh):
    return jax.shard_map(
        functools.partial(local, mesh.shape["tile"], mesh.shape["lev"]),
        mesh=mesh,
        in_specs=(
            P(None, "lev", "tile", None),
            P("lev", "tile", None),
            P("lev", "tile", None),
            P("lev", "tile", None),
            P(None, ("tile", "lev")),
            P(("tile", "lev")),
            P(),
            P(),
            P(),
            P(),
        ),
        out_specs=(P(None, None, ("tile", "lev")), P(None, ("tile", "lev"))),
        check_vma=False,
    )
```
